32 devices in a mesh: groups: 2 (over y), dp: 4 (over x, core), tok: 4 (over z).
Axes of the slice: x: 2, y: 2, z: 4, core: 2. Of those that a mesh axis runs over, the one named last changes fastest.
Arguments:
- train_inputs: bfloat16 [8, 1024, 8192], P(('groups', 'dp'), 'tok'), parts along dimension 0, may hold values from -6 to 6
- train_grads: bfloat16 [8, 1024, 8192], P(('groups', 'dp'), 'tok'), parts along dimension 0, may hold values from -6 to 6
- query_inputs: bfloat16 [16, 1024, 8192], P(('groups', 'dp'), 'tok'), parts along dimension 0, may hold values from -6 to 6
- query_grads: bfloat16 [16, 1024, 8192], P(('groups', 'dp'), 'tok'), parts along dimension 0, may hold values from -6 to 6
- proj_in: bfloat16 [128, 8192], replicated, may hold values from -0.0625 to 0.0625
- proj_out: bfloat16 [128, 8192], replicated, may hold values from -0.0625 to 0.0625
- left_factor: float32 [128, 128], replicated, may hold values from -0.5 to 0.5
- right_factor: float32 [128, 128], replicated, may hold values from -0.5 to 0.5
- train_lengths: int32 [8], P(('groups', 'dp')), parts along dimension 0, may hold values from 128 to 1024, as said below
- train_mask: int32 [8, 1024], P(('groups', 'dp'), 'tok'), parts along dimension 0, may hold values 0 or 1
- query_lengths: int32 [16], P(('groups', 'dp')), parts along dimension 0, may hold values from 128 to 1024, as said below
- query_mask: int32 [16, 1024], P(('groups', 'dp'), 'tok'), parts along dimension 0, may hold values 0 or 1
Outputs:
- scores: float32 [8, 8], P(None, ('groups', 'dp')), parts along dimension 1
The draws below stay inside these ranges and needn't reach their ends.
There are 2 independent parts, one for each index of `groups`. The reference program is written for one: setup_inputs(seed, part) draws one part's arguments, and reference() takes and returns one part's arrays. A program takes and returns all parts, laid end to end along the dimension named above; an argument that names none is the same for every part. Nothing has to cross between parts.
Inputs may be any that keep to these rules, and one draw needn't show every extreme that they name: `train_lengths`: at least one transcript is 1024 long and at least one is 128 long. `query_lengths`: at least one transcript is 1024 long and at least one is 128 long.
All inputs are finite; a program needn't handle non-finite values. No bound on the sum of `train_mask` or of `query_mask` on one device may be relied on, other than what follows from the above.
Results may differ from the reference program's by a relative error of at most 0.0003.
Values sent between devices are 32-bit elements; how exact they have to be, the bound alone decides.
A program may use at most 128 MiB of HBM per device.

```python
import jax
import jax.numpy as jnp
from jax import lax

D = 8192
K = 128
LEN = 1024
N_TRAIN = 4
N_Q = 8


def length_draw(key, count):
    first_key, second_key, third_key = jax.random.split(key, 3)
    values = jax.random.randint(first_key, (count,), LEN // 8, LEN + 1)
    longest = jax.random.randint(second_key, (), 0, count)
    shortest = (longest + 1 + jax.random.randint(third_key, (), 0, count - 1)) % count
    values = values.at[longest].set(LEN)
    values = values.at[shortest].set(LEN // 8)
    return values.astype(jnp.int32)


def draw_train_lengths(key, part):
    key = jax.random.fold_in(key, 11)
    return length_draw(key, N_TRAIN)


def draw_query_lengths(key, part):
    key = jax.random.fold_in(key, 12)
    return length_draw(key, N_Q)


def place_ends(result, key, low, largest):
    index_at = [jax.random.randint(jax.random.fold_in(key, axis), (), 0, length) for axis, length in enumerate(result.shape)]
    widest = result.shape.index(max(result.shape))
    neighbour = index_at[:widest] + [(index_at[widest] + 1) % result.shape[widest]] + index_at[widest + 1:]
    return result.at[tuple(index_at)].set(low).at[tuple(neighbour)].set(largest)


def block_scale(own_key, dims, shards, low, largest):
    gain, own = 1.0, jax.random.fold_in(own_key, 6)
    for position, parts in shards:
        draws = jnp.exp(jax.random.uniform(jax.random.fold_in(own, position), (parts,), jnp.float32, low / len(shards), largest / len(shards)))
        gain = gain * jnp.repeat(draws, dims[position] // parts).reshape([-1 if axis == position else 1 for axis in range(len(dims))])
    return gain


def centred(own_key, shape, deviation, reach, cuts=(), kind=jnp.bfloat16):
    drawn = jax.random.normal(own_key, shape, jnp.float32) * deviation
    if len(cuts) > 0:
        drawn = block_scale(own_key, shape, cuts, -0.22, 0.18) * drawn
    return jnp.clip(drawn, min=-reach, max=reach).astype(kind)


def setup_inputs(seed: int = 0, part: int = 0) -> dict:
    splits = jax.random.split(jax.random.key(seed), 13)
    part_splits = jax.random.split(jax.random.fold_in(splits[12], part), 13)
    train_inputs = centred(part_splits[0], (N_TRAIN, LEN, D), 1.0, 6.0, ((0, 4), (1, 4)))
    train_grads = centred(part_splits[1], (N_TRAIN, LEN, D), 1.0, 6.0, ((0, 4), (1, 4)))
    query_inputs = centred(part_splits[2], (N_Q, LEN, D), 1.0, 6.0, ((0, 4), (1, 4)))
    query_grads = centred(part_splits[3], (N_Q, LEN, D), 1.0, 6.0, ((0, 4), (1, 4)))
    proj_in = centred(splits[4], (K, D), D ** -0.5, 0.0625)
    proj_out = centred(splits[5], (K, D), D ** -0.5, 0.0625)
    left_factor = centred(splits[6], (K, K), K ** -0.5, 0.5, (), jnp.float32)
    right_factor = centred(splits[7], (K, K), K ** -0.5, 0.5, (), jnp.float32)
    train_lengths = draw_train_lengths(jax.random.fold_in(jax.random.fold_in(splits[12], part), 71), part)
    train_mask = place_ends((jax.random.randint(part_splits[9], (N_TRAIN, LEN), 0, 4) < 3).astype(jnp.int32), jax.random.fold_in(part_splits[9], 1), 0, 1)
    query_lengths = draw_query_lengths(jax.random.fold_in(jax.random.fold_in(splits[12], part), 71), part)
    query_mask = place_ends((jax.random.randint(part_splits[11], (N_Q, LEN), 0, 4) < 3).astype(jnp.int32), jax.random.fold_in(part_splits[11], 1), 0, 1)
    return dict(train_inputs=train_inputs, train_grads=train_grads, query_inputs=query_inputs, query_grads=query_grads, proj_in=proj_in, proj_out=proj_out, left_factor=left_factor, right_factor=right_factor, train_lengths=train_lengths, train_mask=train_mask, query_lengths=query_lengths, query_mask=query_mask)


def sketches(inputs, grads, proj_in, proj_out, lengths, mask):
    positions = jnp.arange(LEN, dtype=jnp.int32)

    def single(item):
        rows_in, rows_grad, length, valid = item
        in_proj = jnp.dot(rows_in, proj_in.T, preferred_element_type=jnp.float32)
        out_proj = jnp.dot(rows_grad, proj_out.T, preferred_element_type=jnp.float32)
        weight = (valid * (positions < length).astype(jnp.int32)).astype(jnp.float32)
        total = jnp.dot((out_proj * weight[:, None]).T, in_proj, precision=lax.Precision.HIGHEST)
        return total / jnp.sqrt(length.astype(jnp.float32))
    return lax.map(single, (inputs, grads, lengths, mask))

def reference(train_inputs, train_grads, query_inputs, query_grads, proj_in, proj_out, left_factor, right_factor, train_lengths, train_mask, query_lengths, query_mask):
    train_sketch = sketches(train_inputs, train_grads, proj_in, proj_out, train_lengths, train_mask)
    query_sketch = sketches(query_inputs, query_grads, proj_in, proj_out, query_lengths, query_mask)
    leftside = jnp.matmul(left_factor, query_sketch, precision=lax.Precision.HIGHEST)
    precond = jnp.matmul(leftside, right_factor, precision=lax.Precision.HIGHEST)
    flat_query = precond.reshape(precond.shape[0], K * K)
    flat_train = train_sketch.reshape(train_sketch.shape[0], K * K)
    return jnp.dot(flat_query, flat_train.T, precision=lax.Precision.HIGHEST) / K
```

```python
import functools

import jax
import jax.numpy as jnp
from jax import lax
from jax.experimental import pallas as pl
from jax.experimental.pallas import tpu as pltpu
from jax.sharding import PartitionSpec as P

CHUNKS = 8
MESH = pl.DeviceIdType.MESH
HIGHEST = lax.Precision.HIGHEST


def dot_nt(a, b, precision=None):
    return lax.dot_general(
        a, b, (((1,), (1,)), ((), ())), precision=precision, preferred_element_type=jnp.float32
    )


def kernel(
    n_dp,
    n_tok,
    train_in_hbm,
    train_grad_hbm,
    query_in_hbm,
    query_grad_hbm,
    proj_in_hbm,
    proj_out_hbm,
    left_ref,
    right_ref,
    train_len_ref,
    train_mask_ref,
    query_len_ref,
    query_mask_ref,
    out_ref,
    train_in,
    train_grad,
    query_in,
    query_grad,
    proj_in,
    proj_out,
    acc_a,
    acc_b,
    acc_q,
    weighted,
    part,
    scattered,
    precond,
    own_scores,
    all_scores,
    load_sem,
    scatter_send,
    scatter_recv,
    gather_send,
    gather_recv,
    core_send,
    core_recv,
    score_send,
    score_recv,
):
    n_dev = n_dp * n_tok
    n_half = n_dev // 2
    n_query, tok_rows, width = query_in.shape
    size = proj_in.shape[0]
    cols = width // CHUNKS
    dp, tok = lax.axis_index("dp"), lax.axis_index("tok")
    core, pair = lax.rem(dp, 2), lax.div(dp, 2)
    me = dp * n_tok + tok

    def loads(kind, c):
        span = pl.ds(c * cols, cols)
        pairs = {
            0: (proj_in_hbm.at[:, span], proj_in.at[:, span]),
            1: (train_in_hbm.at[0, :, span], train_in.at[:, span]),
            2: (proj_out_hbm.at[:, span], proj_out.at[:, span]),
            3: (train_grad_hbm.at[0, :, span], train_grad.at[:, span]),
            4: (query_grad_hbm.at[:, :, span], query_grad.at[:, :, span]),
            5: (query_in_hbm.at[:, :, span], query_in.at[:, :, span]),
        }
        return pltpu.make_async_copy(*pairs[kind], load_sem.at[kind, c])

    for c in range(CHUNKS):
        for kind in range(4):
            loads(kind, c).start()
    for kind in (4, 5):
        for c in range(CHUNKS):
            loads(kind, c).start()

    barrier = pltpu.get_barrier_semaphore()
    unroll = n_dev <= 16

    def greet(i, carry):
        other = lax.rem(me + i, n_dev)
        pl.semaphore_signal(
            barrier,
            inc=1,
            device_id={"dp": lax.div(other, n_tok), "tok": lax.rem(other, n_tok)},
            device_id_type=MESH,
        )
        return carry

    lax.fori_loop(1, n_dev, greet, 0, unroll=unroll)

    positions = tok * tok_rows + lax.broadcasted_iota(jnp.int32, (1, tok_rows), 1)

    def weight(mask_row, length):
        lengths = jnp.full((1, tok_rows), length, jnp.int32)
        valid = (mask_row * (positions < lengths).astype(jnp.int32)).astype(jnp.float32)
        return valid / jnp.sqrt(lengths.astype(jnp.float32))

    for c in range(CHUNKS):
        span = pl.ds(c * cols, cols)
        for kind, rows, proj, acc in ((0, train_in, proj_in, acc_a), (2, train_grad, proj_out, acc_b)):
            loads(kind, c).wait()
            loads(kind + 1, c).wait()
            term = dot_nt(rows[:, span], proj[:, span])
            if c == 0:
                acc[...] = term
            else:
                acc[...] += term
    out_t = jnp.transpose(acc_b[...]) * (weight(train_mask_ref[0:1, :], train_len_ref[0]) * (1.0 / size))
    sketch = jnp.dot(out_t, acc_a[...], precision=HIGHEST, preferred_element_type=jnp.float32)
    leftside = jnp.dot(
        jnp.transpose(left_ref[...]), sketch, precision=HIGHEST, preferred_element_type=jnp.float32
    )
    part[...] = dot_nt(leftside, right_ref[...], HIGHEST).reshape(part.shape)

    pl.semaphore_wait(barrier, n_dev - 1)

    def scatter_copy(i):
        other = lax.rem(tok + i, n_tok)
        return pltpu.make_async_remote_copy(
            src_ref=part.at[other],
            dst_ref=scattered.at[tok],
            send_sem=scatter_send,
            recv_sem=scatter_recv,
            device_id={"tok": other},
            device_id_type=MESH,
        )

    for i in range(1, n_tok):
        scatter_copy(i).start()
    scattered[pl.ds(tok, 1)] = part[pl.ds(tok, 1)]

    def bulk(ref, count, send, recv):
        return pltpu.make_async_remote_copy(
            src_ref=ref.at[pl.ds(0, count)],
            dst_ref=ref.at[pl.ds(0, count)],
            send_sem=send,
            recv_sem=recv,
            device_id={"dp": dp},
            device_id_type=MESH,
        )

    def gather_start():
        bulk(scattered, n_tok - 1, scatter_send, scatter_recv).wait_recv()
        precond[pl.ds(me, 1)] = jnp.sum(scattered[...], axis=0, keepdims=True)

        def send(i, carry):
            other = lax.rem(pair * n_tok + tok + i, n_half)
            pltpu.make_async_remote_copy(
                src_ref=precond.at[me],
                dst_ref=precond.at[me],
                send_sem=gather_send,
                recv_sem=gather_recv,
                device_id={"dp": 2 * lax.div(other, n_tok) + core, "tok": lax.rem(other, n_tok)},
                device_id_type=MESH,
            ).start()
            return carry

        lax.fori_loop(1, n_half, send, 0, unroll=unroll)

    def core_start():
        bulk(precond, n_half - 1, gather_send, gather_recv).wait_recv()
        for p in range(n_dp // 2):
            block = precond.at[pl.ds((2 * p + core) * n_tok, n_tok)]
            pltpu.make_async_remote_copy(
                src_ref=block,
                dst_ref=block,
                send_sem=core_send,
                recv_sem=core_recv,
                device_id={"dp": 2 * pair + 1 - core},
                device_id_type=MESH,
            ).start()

    for c in range(CHUNKS):
        span = pl.ds(c * cols, cols)
        loads(4, c).wait()
        term = dot_nt(query_grad[:, :, span].reshape(n_query * tok_rows, cols), proj_out[:, span])
        if c == 0:
            acc_q[...] = term
        else:
            acc_q[...] += term
        if c == 5:
            gather_start()
    for j in range(n_query):
        weighted[j] = jnp.transpose(acc_q[pl.ds(j * tok_rows, tok_rows), :]) * weight(
            query_mask_ref[j : j + 1, :], query_len_ref[j]
        )
    for c in range(CHUNKS):
        span = pl.ds(c * cols, cols)
        loads(5, c).wait()
        term = dot_nt(query_in[:, :, span].reshape(n_query * tok_rows, cols), proj_in[:, span])
        if c == 0:
            acc_q[...] = term
        else:
            acc_q[...] += term
    core_start()
    sketches = [
        jnp.dot(
            weighted[j],
            acc_q[pl.ds(j * tok_rows, tok_rows), :],
            precision=HIGHEST,
            preferred_element_type=jnp.float32,
        )
        for j in range(n_query)
    ]
    bulk(precond, n_half, core_send, core_recv).wait_recv()
    for n in range(n_dp):
        block = precond[pl.ds(n * n_tok, n_tok)].reshape(size, size)
        for j in range(n_query):
            own_scores[n, j : j + 1, :] = jnp.sum(sketches[j] * block, axis=0, keepdims=True)

    def send_scores(i, carry):
        other = lax.rem(me + i, n_dev)
        to_dp, to_tok = lax.div(other, n_tok), lax.rem(other, n_tok)
        pltpu.make_async_remote_copy(
            src_ref=own_scores.at[to_dp],
            dst_ref=all_scores.at[me],
            send_sem=score_send,
            recv_sem=score_recv,
            device_id={"dp": to_dp, "tok": to_tok},
            device_id_type=MESH,
        ).start()
        return carry

    lax.fori_loop(1, n_dev, send_scores, 0, unroll=unroll)
    all_scores[pl.ds(me, 1)] = own_scores[pl.ds(dp, 1)]
    bulk(all_scores, n_dev - 1, score_send, score_recv).wait_recv()
    for d in range(n_dp):
        out_ref[pl.ds(d * n_query, n_query), :] = jnp.sum(all_scores[pl.ds(d * n_tok, n_tok)], axis=0)

    bulk(scattered, n_tok - 1, scatter_send, scatter_recv).wait_send()
    bulk(precond, n_half - 1, gather_send, gather_recv).wait_send()
    bulk(precond, n_half, core_send, core_recv).wait_send()
    bulk(all_scores, n_dev - 1, score_send, score_recv).wait_send()


def per_device(n_dp, n_tok, *args):
    train_inputs, query_inputs, proj_in = args[0], args[2], args[4]
    _, tok_rows, width = train_inputs.shape
    n_query = query_inputs.shape[0]
    size = proj_in.shape[0]
    n_dev = n_dp * n_tok
    rows = size // n_tok
    hbm = pl.BlockSpec(memory_space=pl.ANY)
    vmem = pl.BlockSpec(memory_space=pltpu.VMEM)
    smem = pl.BlockSpec(memory_space=pltpu.SMEM)
    dma = pltpu.SemaphoreType.DMA
    lanes = pl.pallas_call(
        functools.partial(kernel, n_dp, n_tok),
        out_shape=jax.ShapeDtypeStruct((n_dp * n_query, size), jnp.float32),
        in_specs=[hbm] * 6 + [vmem, vmem, smem, vmem, smem, vmem],
        out_specs=vmem,
        scratch_shapes=[
            pltpu.VMEM((tok_rows, width), jnp.bfloat16),
            pltpu.VMEM((tok_rows, width), jnp.bfloat16),
            pltpu.VMEM((n_query, tok_rows, width), jnp.bfloat16),
            pltpu.VMEM((n_query, tok_rows, width), jnp.bfloat16),
            pltpu.VMEM((size, width), jnp.bfloat16),
            pltpu.VMEM((size, width), jnp.bfloat16),
            pltpu.VMEM((tok_rows, size), jnp.float32),
            pltpu.VMEM((tok_rows, size), jnp.float32),
            pltpu.VMEM((n_query * tok_rows, size), jnp.float32),
            pltpu.VMEM((n_query, size, tok_rows), jnp.float32),
            pltpu.VMEM((n_tok, rows, size), jnp.float32),
            pltpu.VMEM((n_tok, rows, size), jnp.float32),
            pltpu.VMEM((n_dev, rows, size), jnp.float32),
            pltpu.VMEM((n_dp, n_query, size), jnp.float32),
            pltpu.VMEM((n_dev, n_query, size), jnp.float32),
            dma((6, CHUNKS)),
            dma,
            dma,
            dma,
            dma,
            dma,
            dma,
            dma,
            dma,
        ],
        compiler_params=pltpu.CompilerParams(
            collective_id=0, has_side_effects=True, vmem_limit_bytes=44 * 1024 * 1024
        ),
        cost_estimate=pl.CostEstimate(
            flops=4 * (1 + n_query) * tok_rows * width * size,
            bytes_accessed=4 * (1 + n_query) * tok_rows * width + 4 * size * width,
            transcendentals=0,
        ),
    )(*args)
    return jnp.sum(lanes, axis=1, keepdims=True)


def solution(mesh):
    n_dp, n_tok = mesh.shape["dp"], mesh.shape["tok"]
    row = P(("groups", "dp"), "tok", None)
    return jax.shard_map(
        functools.partial(per_device, n_dp, n_tok),
        mesh=mesh,
        in_specs=(
            row,
            row,
            row,
            row,
            P(),
            P(),
            P(),
            P(),
            P(("groups", "dp")),
            P(("groups", "dp"), "tok"),
            P(("groups", "dp")),
            P(("groups", "dp"), "tok"),
        ),
        out_specs=P(None, ("groups", "dp")),
        check_vma=False,
    )
```

```python
import functools

import jax
import jax.numpy as jnp
from jax import lax
from jax.experimental import pallas as pl
from jax.experimental.pallas import tpu as pltpu
from jax.sharding import PartitionSpec as P

CHUNKS = 4
WINDOW = 6
MESH = pl.DeviceIdType.MESH
HIGHEST = lax.Precision.HIGHEST


def dot_nt(a, b, precision=None):
    return lax.dot_general(
        a, b, (((1,), (1,)), ((), ())), precision=precision, preferred_element_type=jnp.float32
    )


def kernel(
    n_dp,
    n_tok,
    train_in_hbm,
    train_grad_hbm,
    query_in_hbm,
    query_grad_hbm,
    proj_in_hbm,
    proj_out_hbm,
    left_hbm,
    right_hbm,
    train_len_hbm,
    train_mask_hbm,
    query_len_hbm,
    query_mask_hbm,
    out_ref,
    train_in,
    train_grad,
    query_in,
    query_grad,
    proj_in,
    proj_out,
    acc_a,
    acc_b,
    acc_q,
    weighted,
    part,
    scattered,
    precond,
    own_scores,
    all_scores,
    left_ref,
    right_ref,
    train_len_ref,
    train_mask_ref,
    query_len_ref,
    query_mask_ref,
    load_sem,
    small_sem,
    scatter_send,
    scatter_recv,
    gather_send,
    gather_recv,
    core_send,
    core_recv,
    score_send,
    score_recv,
):
    n_dev = n_dp * n_tok
    n_half = n_dev // 2
    n_query, tok_rows, width = query_in.shape
    size = proj_in.shape[0]
    cols = width // CHUNKS
    dp, tok = lax.axis_index("dp"), lax.axis_index("tok")
    core, pair = lax.rem(dp, 2), lax.div(dp, 2)
    me = dp * n_tok + tok

    def loads(kind, c):
        span = pl.ds(c * cols, cols)
        pairs = {
            0: (proj_in_hbm.at[:, span], proj_in.at[:, span]),
            1: (train_in_hbm.at[0, :, span], train_in.at[:, span]),
            2: (proj_out_hbm.at[:, span], proj_out.at[:, span]),
            3: (train_grad_hbm.at[0, :, span], train_grad.at[:, span]),
            4: (query_grad_hbm.at[:, :, span], query_grad.at[:, :, span]),
            5: (query_in_hbm.at[:, :, span], query_in.at[:, :, span]),
        }
        return pltpu.make_async_copy(*pairs[kind], load_sem.at[kind, c])

    order = [(kind, c) for c in range(CHUNKS) for kind in range(4)]
    order += [(4, c) for c in range(CHUNKS)] + [(5, c) for c in range(CHUNKS)]
    for load in order[:WINDOW]:
        loads(*load).start()

    def fetch(*load):
        loads(*load).wait()
        ahead = order.index(load) + WINDOW
        if ahead < len(order):
            loads(*order[ahead]).start()

    small = [
        pltpu.make_async_copy(src, dst, small_sem.at[i])
        for i, (src, dst) in enumerate(
            (
                (left_hbm, left_ref),
                (right_hbm, right_ref),
                (train_len_hbm, train_len_ref),
                (train_mask_hbm, train_mask_ref),
                (query_len_hbm, query_len_ref),
                (query_mask_hbm, query_mask_ref),
            )
        )
    ]
    for copy in small:
        copy.start()

    barrier = pltpu.get_barrier_semaphore()
    unroll = n_dev <= 16

    def greet(i, carry):
        other = lax.rem(me + i, n_dev)
        pl.semaphore_signal(
            barrier,
            inc=1,
            device_id={"dp": lax.div(other, n_tok), "tok": lax.rem(other, n_tok)},
            device_id_type=MESH,
        )
        return carry

    lax.fori_loop(1, n_dev, greet, 0, unroll=unroll)

    positions = tok * tok_rows + lax.broadcasted_iota(jnp.int32, (1, tok_rows), 1)

    def weight(mask_row, length):
        lengths = jnp.full((1, tok_rows), length, jnp.int32)
        valid = (mask_row * (positions < lengths).astype(jnp.int32)).astype(jnp.float32)
        return valid / jnp.sqrt(lengths.astype(jnp.float32))

    for c in range(CHUNKS):
        span = pl.ds(c * cols, cols)
        for kind, rows, proj, acc in ((0, train_in, proj_in, acc_a), (2, train_grad, proj_out, acc_b)):
            fetch(kind, c)
            fetch(kind + 1, c)
            term = dot_nt(proj[:, span], rows[:, span])
            if c == 0:
                acc[...] = term
            else:
                acc[...] += term
    for copy in small:
        copy.wait()
    out_t = acc_b[...] * (weight(train_mask_ref[0:1, :], train_len_ref[0]) * (1.0 / size))
    sketch = dot_nt(out_t, acc_a[...], HIGHEST)
    leftside = jnp.dot(
        jnp.transpose(left_ref[...]), sketch, precision=HIGHEST, preferred_element_type=jnp.float32
    )
    part[...] = dot_nt(leftside, right_ref[...], HIGHEST).reshape(part.shape)

    pl.semaphore_wait(barrier, n_dev - 1)

    def scatter_copy(i):
        other = lax.rem(tok + i, n_tok)
        return pltpu.make_async_remote_copy(
            src_ref=part.at[other],
            dst_ref=scattered.at[tok],
            send_sem=scatter_send,
            recv_sem=scatter_recv,
            device_id={"tok": other},
            device_id_type=MESH,
        )

    for i in range(1, n_tok):
        scatter_copy(i).start()
    scattered[pl.ds(tok, 1)] = part[pl.ds(tok, 1)]

    def bulk(ref, count, send, recv):
        return pltpu.make_async_remote_copy(
            src_ref=ref.at[pl.ds(0, count)],
            dst_ref=ref.at[pl.ds(0, count)],
            send_sem=send,
            recv_sem=recv,
            device_id={"dp": dp},
            device_id_type=MESH,
        )

    def gather_start():
        bulk(scattered, n_tok - 1, scatter_send, scatter_recv).wait_recv()
        precond[pl.ds(me, 1)] = jnp.sum(scattered[...], axis=0, keepdims=True)

        def send(i, carry):
            other = lax.rem(pair * n_tok + tok + i, n_half)
            pltpu.make_async_remote_copy(
                src_ref=precond.at[me],
                dst_ref=precond.at[me],
                send_sem=gather_send,
                recv_sem=gather_recv,
                device_id={"dp": 2 * lax.div(other, n_tok) + core, "tok": lax.rem(other, n_tok)},
                device_id_type=MESH,
            ).start()
            return carry

        lax.fori_loop(1, n_half, send, 0, unroll=unroll)

    def core_start():
        bulk(precond, n_half - 1, gather_send, gather_recv).wait_recv()
        for p in range(n_dp // 2):
            block = precond.at[pl.ds((2 * p + core) * n_tok, n_tok)]
            pltpu.make_async_remote_copy(
                src_ref=block,
                dst_ref=block,
                send_sem=core_send,
                recv_sem=core_recv,
                device_id={"dp": 2 * pair + 1 - core},
                device_id_type=MESH,
            ).start()

    for c in range(CHUNKS):
        span = pl.ds(c * cols, cols)
        fetch(4, c)
        term = dot_nt(proj_out[:, span], query_grad[:, :, span].reshape(n_query * tok_rows, cols))
        if c == 0:
            acc_q[...] = term
        else:
            acc_q[...] += term
        if c == 3:
            gather_start()
    for j in range(n_query):
        weighted[j] = acc_q[:, pl.ds(j * tok_rows, tok_rows)] * weight(
            query_mask_ref[j : j + 1, :], query_len_ref[j]
        )
    for c in range(CHUNKS):
        span = pl.ds(c * cols, cols)
        fetch(5, c)
        term = dot_nt(proj_in[:, span], query_in[:, :, span].reshape(n_query * tok_rows, cols))
        if c == 0:
            acc_q[...] = term
        else:
            acc_q[...] += term
    core_start()
    sketches = [
        dot_nt(weighted[j], acc_q[:, pl.ds(j * tok_rows, tok_rows)], HIGHEST)
        for j in range(n_query)
    ]
    bulk(precond, n_half, core_send, core_recv).wait_recv()
    for n in range(n_dp):
        block = precond[pl.ds(n * n_tok, n_tok)].reshape(size, size)
        for j in range(n_query):
            own_scores[n, j : j + 1, :] = jnp.sum(sketches[j] * block, axis=0, keepdims=True)

    def send_scores(i, carry):
        other = lax.rem(me + i, n_dev)
        to_dp, to_tok = lax.div(other, n_tok), lax.rem(other, n_tok)
        pltpu.make_async_remote_copy(
            src_ref=own_scores.at[to_dp],
            dst_ref=all_scores.at[me],
            send_sem=score_send,
            recv_sem=score_recv,
            device_id={"dp": to_dp, "tok": to_tok},
            device_id_type=MESH,
        ).start()
        return carry

    lax.fori_loop(1, n_dev, send_scores, 0, unroll=unroll)
    all_scores[pl.ds(me, 1)] = own_scores[pl.ds(dp, 1)]
    bulk(all_scores, n_dev - 1, score_send, score_recv).wait_recv()
    for d in range(n_dp):
        out_ref[pl.ds(d * n_query, n_query), :] = jnp.sum(all_scores[pl.ds(d * n_tok, n_tok)], axis=0)

    bulk(scattered, n_tok - 1, scatter_send, scatter_recv).wait_send()
    bulk(precond, n_half - 1, gather_send, gather_recv).wait_send()
    bulk(precond, n_half, core_send, core_recv).wait_send()
    bulk(all_scores, n_dev - 1, score_send, score_recv).wait_send()


def per_device(n_dp, n_tok, *args):
    train_inputs, query_inputs, proj_in = args[0], args[2], args[4]
    _, tok_rows, width = train_inputs.shape
    n_query = query_inputs.shape[0]
    size = proj_in.shape[0]
    n_dev = n_dp * n_tok
    rows = size // n_tok
    hbm = pl.BlockSpec(memory_space=pltpu.HBM)
    vmem = pl.BlockSpec(memory_space=pltpu.VMEM)
    dma = pltpu.SemaphoreType.DMA
    lanes = pl.pallas_call(
        functools.partial(kernel, n_dp, n_tok),
        out_shape=jax.ShapeDtypeStruct((n_dp * n_query, size), jnp.float32),
        in_specs=[hbm] * 12,
        out_specs=vmem,
        scratch_shapes=[
            pltpu.VMEM((tok_rows, width), jnp.bfloat16),
            pltpu.VMEM((tok_rows, width), jnp.bfloat16),
            pltpu.VMEM((n_query, tok_rows, width), jnp.bfloat16),
            pltpu.VMEM((n_query, tok_rows, width), jnp.bfloat16),
            pltpu.VMEM((size, width), jnp.bfloat16),
            pltpu.VMEM((size, width), jnp.bfloat16),
            pltpu.VMEM((size, tok_rows), jnp.float32),
            pltpu.VMEM((size, tok_rows), jnp.float32),
            pltpu.VMEM((size, n_query * tok_rows), jnp.float32),
            pltpu.VMEM((n_query, size, tok_rows), jnp.float32),
            pltpu.VMEM((n_tok, rows, size), jnp.float32),
            pltpu.VMEM((n_tok, rows, size), jnp.float32),
            pltpu.VMEM((n_dev, rows, size), jnp.float32),
            pltpu.VMEM((n_dp, n_query, size), jnp.float32),
            pltpu.VMEM((n_dev, n_query, size), jnp.float32),
            *[(pltpu.SMEM if x.ndim == 1 else pltpu.VMEM)(x.shape, x.dtype) for x in args[6:]],
            dma((6, CHUNKS)),
            dma((6,)),
            dma,
            dma,
            dma,
            dma,
            dma,
            dma,
            dma,
            dma,
        ],
        compiler_params=pltpu.CompilerParams(
            collective_id=0, has_side_effects=True, vmem_limit_bytes=62 * 1024 * 1024
        ),
        cost_estimate=pl.CostEstimate(
            flops=4 * (1 + n_query) * tok_rows * width * size,
            bytes_accessed=4 * (1 + n_query) * tok_rows * width + 4 * size * width,
            transcendentals=0,
        ),
    )(*args)
    return jnp.sum(lanes, axis=1, keepdims=True)


def solution(mesh):
    n_dp, n_tok = mesh.shape["dp"], mesh.shape["tok"]
    row = P(("groups", "dp"), "tok", None)
    return jax.shard_map(
        functools.partial(per_device, n_dp, n_tok),
        mesh=mesh,
        in_specs=(
            row,
            row,
            row,
            row,
            P(),
            P(),
            P(),
            P(),
            P(("groups", "dp")),
            P(("groups", "dp"), "tok"),
            P(("groups", "dp")),
            P(("groups", "dp"), "tok"),
        ),
        out_specs=P(None, ("groups", "dp")),
        check_vma=False,
    )
```
